512 devices in a mesh: dp: 16 (over x, y), seq: 32 (over z, core).
Axes of the slice: x: 4, y: 4, z: 16, core: 2. Of those that a mesh axis runs over, the one named last changes fastest.
Arguments:
- queries: bfloat16 [16, 768, 2048], P('dp', 'seq'), may hold values from -18 to 18
- keys: bfloat16 [16, 8192, 2048], P('dp', 'seq'), may hold values from -18 to 18
- values: bfloat16 [16, 8192, 2048], P('dp', 'seq'), may hold values from -6 to 6
- attn_out: bfloat16 [16, 768, 2048], P('dp', 'seq'), may hold values from -3 to 3
- out_grad: bfloat16 [16, 768, 2048], P('dp', 'seq'), may hold values from -12 to 12
- loss_mask: int32 [16, 768], P('dp', 'seq'), may hold values from 0 to 1, as said below
- input_lengths: int32 [16, 1, 4], P('dp'), may hold values from 1 to 4096, 8192 in all within a row
- target_lengths: int32 [16, 1, 4], P('dp'), may hold values from 1 to 384, 768 in all within a row
Outputs:
- grad_queries: bfloat16 [16, 768, 2048], P('dp', 'seq')
- grad_keys: bfloat16 [16, 8192, 2048], P('dp', 'seq')
- grad_values: bfloat16 [16, 8192, 2048], P('dp', 'seq')
The draws below stay inside these ranges and needn't reach their ends.
Inputs may be any that keep to these rules, and one draw needn't show every extreme that they name: `loss_mask`: the first of each device's 24 target rows carries loss.
All inputs are finite; a program needn't handle non-finite values.
Results may differ from the reference program's by a relative error of at most 0.0095.
Values may be sent and summed in bfloat16 or wider, within the bound.
A program may use at most 128 MiB of HBM per device.

```python
import math
import jax
import jax.numpy as jnp
import numpy as np
from jax import lax

HEADS = 8
HEAD_SIZE = 256
FEATURES = 2048
ENC_DEV = 256
DEC_DEV = 24
BLOCK = 32
DOCS = 4
BLOCKS = 1
ENC_ROWS = 8192
DEC_ROWS = 768
MOST_IN = 4096
MOST_OUT = 384
N_DP = 16


def draw_queries(key, part):
    key = jax.random.fold_in(key, 11)
    full_shape = (N_DP, DEC_ROWS, HEADS * HEAD_SIZE)
    drawn_values = jnp.clip(jax.random.normal(key, full_shape, jnp.float32), -6.0, 6.0)
    return drawn_values.astype(jnp.bfloat16)


def draw_keys(key, part):
    key = jax.random.fold_in(key, 13)
    full_shape = (N_DP, ENC_ROWS, HEADS * HEAD_SIZE)
    drawn_values = jnp.clip(jax.random.normal(key, full_shape, jnp.float32), -6.0, 6.0)
    return drawn_values.astype(jnp.bfloat16)


def draw_loss_mask(key, part):
    key = jax.random.fold_in(key, 23)
    per_group = DEC_ROWS // DEC_DEV
    device_count = N_DP * per_group
    row_index = lax.broadcasted_iota(jnp.int32, (N_DP, DEC_ROWS), 1)
    group_index = lax.broadcasted_iota(jnp.int32, (N_DP, DEC_ROWS), 0)
    device_index = group_index * per_group + row_index // DEC_DEV
    threshold = 250 + 500 * device_index // max(device_count - 1, 1)
    drawn_values = jax.random.randint(key, (N_DP, DEC_ROWS), 0, 1000)
    carries = (drawn_values < threshold) | (row_index % DEC_DEV == 0)
    return jnp.where(carries, 1, 0).astype(jnp.int32)


def block_levels(own_key, dims, cuts, smallest, high):
    loudness, own = 1.0, jax.random.fold_in(own_key, 6)
    for position, shards_of in cuts:
        heights = jnp.exp(jax.random.uniform(jax.random.fold_in(own, position), (shards_of,), jnp.float32, smallest / len(cuts), high / len(cuts)))
        loudness = loudness * jnp.repeat(heights, dims[position] // shards_of).reshape([-1 if axis == position else 1 for axis in range(len(dims))])
    return loudness


def split_up(count, total, limit, skew):
    portions = [(1 << 20) // math.isqrt(standing ** skew) + 1 for standing in range(2, count + 1)]
    rest, given = total - limit - (count - 1), [1] * (count - 1)
    while rest > 0:
        candidates = [i for i in range(count - 1) if given[i] < limit]
        whole, remaining = sum([portions[i] for i in candidates]), rest
        for i in candidates:
            addition = min(limit - given[i], max(1, remaining * portions[i] // whole), rest)
            given[i] = given[i] + addition
            rest = rest - addition
    return np.array([limit] + given)


def uneven_parts(rng, number_of, total, most, lean):
    if number_of == 2:
        one = jax.random.randint(rng, (), max(1, total - most), min(most, total - 1) + 1)
        return jnp.stack([one, total - one])
    sizes = jnp.asarray(split_up(number_of, total, most, lean), jnp.int32)
    couples = (number_of - 1) // 2
    donor, receiver = sizes[1:1 + 2 * couples:2], sizes[2:2 + 2 * couples:2]
    room = jnp.minimum(donor - 1, most - receiver)
    moved = jax.random.randint(jax.random.fold_in(rng, 1), (couples,), 0, 1 << 20) % (room + 1)
    sizes = sizes.at[1:1 + 2 * couples:2].set(donor - moved).at[2:2 + 2 * couples:2].set(receiver + moved)
    return sizes[jax.random.permutation(jax.random.fold_in(rng, 2), number_of)]


def normal_values(stream_key, shape, deviation, most, pieces=(), held_as=jnp.bfloat16):
    array = jax.random.normal(stream_key, shape, jnp.float32) * deviation
    if len(pieces) > 0:
        array = block_levels(stream_key, shape, pieces, -0.22, 0.18) * array
    return jnp.clip(array, min=-most, max=most).astype(held_as)


def setup_inputs(seed: int = 0) -> dict:
    streams_of = jax.random.split(jax.random.key(seed), 9)
    queries = draw_queries(jax.random.fold_in(streams_of[8], 71), 0)
    keys = draw_keys(jax.random.fold_in(streams_of[8], 71), 0)
    values = normal_values(streams_of[2], (N_DP, ENC_ROWS, FEATURES), 1.0, 6.0, ((0, 16), (1, 32)))
    attn_out = normal_values(streams_of[3], (N_DP, DEC_ROWS, FEATURES), 0.5, 3.0, ((0, 16), (1, 32)))
    out_grad = normal_values(streams_of[4], (N_DP, DEC_ROWS, FEATURES), 2.0, 12.0, ((0, 16), (1, 32)))
    loss_mask = draw_loss_mask(jax.random.fold_in(streams_of[8], 71), 0)
    input_lengths = jax.vmap(lambda own: uneven_parts(own, DOCS, BLOCK * ENC_DEV, MOST_IN, 2))(jax.random.split(streams_of[6], N_DP * BLOCKS)).reshape((N_DP, BLOCKS, DOCS)).astype(jnp.int32)
    target_lengths = jax.vmap(lambda own: uneven_parts(own, DOCS, BLOCK * DEC_DEV, MOST_OUT, 2))(jax.random.split(streams_of[7], N_DP * BLOCKS)).reshape((N_DP, BLOCKS, DOCS)).astype(jnp.int32)
    return {"queries": queries, "keys": keys, "values": values, "attn_out": attn_out, "out_grad": out_grad, "loss_mask": loss_mask, "input_lengths": input_lengths, "target_lengths": target_lengths}


def document_ids(lengths, positions):
    doc_ends = jnp.cumsum(lengths)
    return jnp.sum((positions[:, None] >= doc_ends[None, :]).astype(jnp.int32), axis=1)


def block_grads(block_inputs):
    query_rows, key_rows, value_rows, grad_rows, delta_rows, input_lens, target_lens = block_inputs
    dec_count = query_rows.shape[0]
    enc_count = key_rows.shape[0]
    enc_doc = document_ids(input_lens, jnp.arange(enc_count, dtype=jnp.int32))
    dec_doc = document_ids(target_lens, jnp.arange(dec_count, dtype=jnp.int32))
    allowed = dec_doc[:, None] == enc_doc[None, :]
    inverse_root = HEAD_SIZE ** -0.5
    query_heads = query_rows.astype(jnp.float32).reshape(dec_count, HEADS, HEAD_SIZE)
    key_heads = key_rows.astype(jnp.float32).reshape(enc_count, HEADS, HEAD_SIZE)
    value_heads = value_rows.astype(jnp.float32).reshape(enc_count, HEADS, HEAD_SIZE)
    grad_heads = grad_rows.astype(jnp.float32).reshape(dec_count, HEADS, HEAD_SIZE)
    scores = jnp.einsum('rhd,ehd->hre', query_heads, key_heads) * inverse_root
    masked_scores = jnp.where(allowed[None], scores, -1e30)
    row_top = jnp.max(masked_scores, axis=2)
    row_total = jnp.sum(jnp.where(allowed[None], jnp.exp(scores - row_top[:, :, None]), 0.0), axis=2)
    log_total = row_top + jnp.log(row_total)
    probs = jnp.where(allowed[None], jnp.exp(scores - log_total[:, :, None]), 0.0)
    dprob = jnp.einsum('rhd,ehd->hre', grad_heads, value_heads)
    dscore = probs * (dprob - delta_rows.astype(jnp.float32).T[:, :, None])
    probs_low = probs.astype(jnp.bfloat16).astype(jnp.float32)
    dscore_low = dscore.astype(jnp.bfloat16).astype(jnp.float32)
    dvalue = jnp.einsum('hre,rhd->ehd', probs_low, grad_heads).reshape(enc_count, HEADS * HEAD_SIZE)
    dkey = jnp.einsum('hre,rhd->ehd', dscore_low, query_heads).reshape(enc_count, HEADS * HEAD_SIZE) * inverse_root
    dquery = jnp.einsum('hre,ehd->rhd', dscore_low, key_heads).reshape(dec_count, HEADS * HEAD_SIZE) * inverse_root
    return dquery, dkey, dvalue


def reference(queries, keys, values, attn_out, out_grad, loss_mask, input_lengths, target_lengths):
    features = HEADS * HEAD_SIZE
    masked = out_grad * loss_mask[:, :, None].astype(jnp.bfloat16)
    delta = jnp.sum((masked.astype(jnp.float32) * attn_out.astype(jnp.float32)).reshape(N_DP, DEC_ROWS, HEADS, HEAD_SIZE), axis=3).astype(jnp.bfloat16)
    count = jnp.sum(loss_mask).astype(jnp.float32)
    factor = jnp.float32(N_DP * DEC_ROWS) / count
    block_count = N_DP * BLOCKS
    dec_block = BLOCK * DEC_DEV
    enc_block = BLOCK * ENC_DEV
    stacked = (queries.reshape(block_count, dec_block, features),
               keys.reshape(block_count, enc_block, features),
               values.reshape(block_count, enc_block, features),
               masked.reshape(block_count, dec_block, features),
               delta.reshape(block_count, dec_block, HEADS),
               input_lengths.reshape(block_count, DOCS),
               target_lengths.reshape(block_count, DOCS))
    dquery, dkey, dvalue = lax.map(block_grads, stacked)
    grad_queries = (factor * dquery).astype(jnp.bfloat16).reshape(N_DP, DEC_ROWS, features)
    grad_keys = (factor * dkey).astype(jnp.bfloat16).reshape(N_DP, ENC_ROWS, features)
    grad_values = (factor * dvalue).astype(jnp.bfloat16).reshape(N_DP, ENC_ROWS, features)
    return grad_queries, grad_keys, grad_values
```

```python
import functools

import jax
import jax.numpy as jnp
from jax import lax
from jax.experimental import pallas as pl
from jax.experimental.pallas import tpu as pltpu
from jax.sharding import PartitionSpec as P

HEADS = 8
HEAD_SIZE = 256
HALF_HEADS = HEADS // 2
HALF = HALF_HEADS * HEAD_SIZE
LANES = 128
CHUNKS = 2
LAG = 4
NEVER = -1e30
MESH = pl.DeviceIdType.MESH


def nt(a, b):
    return lax.dot_general(a, b, (((1,), (1,)), ((), ())), preferred_element_type=jnp.float32)


def tn(a, b):
    return lax.dot_general(a, b, (((0,), (0,)), ((), ())), preferred_element_type=jnp.float32)


def nn(a, b):
    return jnp.dot(a, b, preferred_element_type=jnp.float32)


def kernel(
    dp_x,
    dp_y,
    chips,
    in_len,
    out_len,
    q_ref,
    g_ref,
    a_ref,
    mask_ref,
    k_ref,
    v_ref,
    dq_ref,
    dk_ref,
    dv_ref,
    stage_out,
    stage_in,
    kx,
    vx,
    qb,
    mb,
    kdoc,
    scores,
    probs,
    dscores,
    dq_part,
    rs_in,
    rs_out,
    grads,
    fin,
    fin_in,
    tile_out,
    tile_in,
    log_out,
    log_in,
    row_info,
    count_out,
    count_in,
    kv_local,
    kv_send,
    kv_recv,
    stage_send,
    stage_recv,
    ag_send,
    ag_recv,
    rs_send,
    rs_recv,
    tile_send,
    tile_recv,
    log_send,
    log_recv,
    count_send,
    count_recv,
    out_local,
    out_send,
    out_recv,
    fin_send,
    fin_recv,
):
    rows = q_ref.shape[0]
    keys_dev = k_ref.shape[0]
    block = 2 * rows
    keys_chip = 2 * keys_dev
    slots = chips // 2
    wide = HALF // CHUNKS
    dp = lax.axis_index("dp")
    seq = lax.axis_index("seq")
    z = seq // 2
    core = seq % 2
    sibling = (dp, z * 2 + 1 - core)

    def chip_at(offset):
        return (dp, ((z + offset + chips) % chips) * 2 + core)

    ahead = (chip_at(1), chip_at(-1))
    peers_x = [((dp + dp_y * k) % (dp_x * dp_y), seq) for k in range(1, dp_x)]
    peers_y = [((dp // dp_y) * dp_y + (dp % dp_y + k) % dp_y, seq) for k in range(1, dp_y)]

    mine = pl.ds(pl.multiple_of(core * HALF, HALF), HALF)
    theirs = pl.ds(pl.multiple_of((1 - core) * HALF, HALF), HALF)
    my_keys = pl.ds(pl.multiple_of(core * keys_dev, keys_dev), keys_dev)
    their_keys = pl.ds(pl.multiple_of((1 - core) * keys_dev, keys_dev), keys_dev)

    def remote(src, dst, send, recv, device):
        return pltpu.make_async_remote_copy(
            src_ref=src, dst_ref=dst, send_sem=send, recv_sem=recv, device_id=device, device_id_type=MESH
        )

    kv_own = [
        pltpu.make_async_copy(ref.at[:, mine], buf.at[my_keys], kv_local.at[i])
        for i, (ref, buf) in enumerate(((k_ref, kx), (v_ref, vx)))
    ]
    kv_sent = [
        remote(ref.at[:, theirs], buf.at[my_keys], kv_send.at[i], kv_recv.at[i], sibling)
        for i, (ref, buf) in enumerate(((k_ref, kx), (v_ref, vx)))
    ]
    staged = [
        remote(stage_out.at[i], stage_in.at[i], stage_send.at[i], stage_recv.at[i], sibling) for i in range(3)
    ]
    count_swap = remote(count_out.at[2], count_in.at[2, 0], stage_send.at[3], stage_recv.at[3], sibling)

    def gathered(which, way, hop, chunk):
        buf = (qb, mb)[which]
        source = hop * LANES + (way * block if hop else 0)
        target = block if hop == slots - 1 else (hop + 1) * LANES + way * block
        columns = pl.ds(chunk * wide, wide)
        return remote(
            buf.at[pl.ds(source, block), columns],
            buf.at[pl.ds(target, block), columns],
            ag_send.at[which, way, hop, chunk],
            ag_recv.at[which, way, hop, chunk],
            ahead[way],
        )

    def chunks_of_hop(way, hop, last):
        if hop != last:
            return range(CHUNKS)
        return range(CHUNKS // 2) if way == 0 else range(CHUNKS // 2, CHUNKS)

    def forward(which, hop):
        for chunk in range(CHUNKS):
            for way in range(2):
                if chunk in chunks_of_hop(way, hop, slots - 1):
                    gathered(which, way, hop, chunk).wait_recv()
                    if hop + 1 < slots and chunk in chunks_of_hop(way, hop + 1, slots - 1):
                        gathered(which, way, hop + 1, chunk).start()

    def scattered(way, hop, chunk):
        columns = pl.ds(chunk * wide, wide)
        return remote(
            rs_out.at[way, hop, :, columns],
            rs_in.at[way, hop, :, columns],
            rs_send.at[way, hop, chunk],
            rs_recv.at[way, hop, chunk],
            ahead[way],
        )

    def tile_copies(slot):
        if slot == 0:
            return [remote(tile_out.at[0], tile_in.at[slots], tile_send.at[slots], tile_recv.at[slots], chip_at(slots))]
        return [
            remote(tile_out.at[slot], tile_in.at[slot], tile_send.at[slot], tile_recv.at[slot], chip_at(-slot)),
            remote(
                tile_out.at[slot],
                tile_in.at[slots + slot],
                tile_send.at[slots + slot],
                tile_recv.at[slots + slot],
                chip_at(slot),
            ),
        ]

    def log_copy(offset):
        return remote(log_out, log_in.at[offset], log_send.at[offset], log_recv.at[offset], chip_at(offset))

    def count_copy(phase, k, device):
        return remote(
            count_out.at[phase], count_in.at[phase, k], count_send.at[phase, k], count_recv.at[phase, k], device
        )

    def grad_copies(which, head):
        out = (dk_ref, dv_ref)[which]
        columns = pl.ds(head * HEAD_SIZE, HEAD_SIZE)
        target = pl.ds(pl.multiple_of(core * HALF + head * HEAD_SIZE, HEAD_SIZE), HEAD_SIZE)
        return [
            pltpu.make_async_copy(
                grads.at[which, my_keys, columns], out.at[:, target], out_local.at[which, head]
            ),
            remote(
                grads.at[which, their_keys, columns],
                out.at[:, target],
                out_send.at[which, head],
                out_recv.at[which, head],
                sibling,
            ),
        ]

    for copy in kv_own:
        copy.start()
    barrier = pltpu.get_barrier_semaphore()
    greeted = [sibling, *ahead, *peers_x, *peers_y]
    for device in greeted:
        pl.semaphore_signal(barrier, inc=1, device_id=device, device_id_type=MESH)

    mask_row = mask_ref[...]
    eye = lax.broadcasted_iota(jnp.int32, (rows, rows), 0) == lax.broadcasted_iota(jnp.int32, (rows, rows), 1)
    mask_column = jnp.sum(jnp.where(eye, mask_row, 0), axis=1, keepdims=True).astype(jnp.float32)
    count_out[2] = jnp.full((8, LANES), jnp.sum(mask_row).astype(jnp.float32))
    stage_out[0] = q_ref[:, theirs].astype(jnp.float32)
    pl.semaphore_wait(barrier, len(greeted))
    staged[0].start()
    stage_out[1] = g_ref[:, theirs].astype(jnp.float32) * mask_column
    staged[1].start()
    stage_out[2] = a_ref[:, theirs].astype(jnp.float32)
    staged[2].start()
    count_swap.start()
    for copy in kv_sent:
        copy.start()

    def both(own, other):
        return jnp.concatenate([jnp.where(core == 0, own, other), jnp.where(core == 0, other, own)], axis=0)

    staged[0].wait_recv()
    qb[0:block, :] = both(q_ref[:, mine].astype(jnp.float32), stage_in[0]).astype(jnp.bfloat16)
    for chunk in range(CHUNKS):
        for way in range(2):
            if chunk in chunks_of_hop(way, 0, slots - 1):
                gathered(0, way, 0, chunk).start()
    staged[1].wait_recv()
    masked = both(g_ref[:, mine].astype(jnp.float32) * mask_column, stage_in[1])
    mb[0:block, :] = masked.astype(jnp.bfloat16)

    staged[2].wait_recv()
    product = masked * both(a_ref[:, mine].astype(jnp.float32), stage_in[2])
    product = jnp.concatenate([product, jnp.zeros((LANES - block, HALF), jnp.float32)], axis=0)
    high = product.astype(jnp.bfloat16)
    low = (product - high.astype(jnp.float32)).astype(jnp.bfloat16)
    head_of = lax.broadcasted_iota(jnp.int32, (8, HALF), 1) // HEAD_SIZE
    picks = (head_of == lax.broadcasted_iota(jnp.int32, (8, HALF), 0) - HALF_HEADS).astype(jnp.bfloat16)
    delta = (nt(picks, high) + nt(picks, low)).astype(jnp.bfloat16).astype(jnp.float32)

    for slot in range(slots):
        for buf in (qb, mb):
            buf[slot * LANES + 2 * block : (slot + 1) * LANES, :] = jnp.zeros(
                (LANES - 2 * block, HALF), jnp.bfloat16
            )

    ends = [in_len[0]]
    row_ends = [out_len[0]]
    for d in range(1, 3):
        ends.append(ends[-1] + in_len[d])
        row_ends.append(row_ends[-1] + out_len[d])
    key_at = z * keys_chip + lax.broadcasted_iota(jnp.int32, (keys_chip, LANES), 0)
    kdoc[...] = sum((key_at >= end).astype(jnp.int32) for end in ends)
    lane = lax.broadcasted_iota(jnp.int32, (1, LANES), 1)

    count_swap.wait_recv()
    chip_count = count_out[2] + count_in[2, 0]

    for copy in (kv_own[0], kv_own[1]):
        copy.wait()
    kv_sent[0].wait_recv()

    def score_slot(slot):
        left = (z - slot + chips) % chips
        right = (z + (slot if slot else slots)) % chips
        at = jnp.where(lane < block, left * block + lane, right * block + lane - block)
        doc = sum((at >= end).astype(jnp.int32) for end in row_ends)
        doc = jnp.where(lane < 2 * block, doc, -1)
        for head in range(HALF_HEADS):
            columns = slice(head * HEAD_SIZE, (head + 1) * HEAD_SIZE)
            s = nt(kx[:, columns], qb[slot * LANES : (slot + 1) * LANES, columns]) * HEAD_SIZE ** (-0.5)
            s = jnp.where(kdoc[...] == doc, s, NEVER)
            scores[slot, head] = s
            top = jnp.max(s, axis=0, keepdims=True)
            tile_out[slot, head : head + 1] = top + jnp.log(jnp.sum(jnp.exp(s - top), axis=0, keepdims=True))
        tile_out[slot, HALF_HEADS:] = chip_count[HALF_HEADS:]
        for copy in tile_copies(slot):
            copy.start()

    def combine_logs():
        for slot in range(slots):
            for copy in tile_copies(slot):
                copy.wait_recv()
        tiles = [tile_out[0]] + [tile_in[i] for i in range(1, slots)]
        tiles += [pltpu.roll(tile_in[i], LANES - block, 1) for i in range(slots, chips)]
        top = functools.reduce(jnp.maximum, tiles)
        total = top + jnp.log(sum(jnp.exp(tile - top) for tile in tiles))
        upper = lax.broadcasted_iota(jnp.int32, (8, LANES), 0) < HALF_HEADS
        log_out[...] = jnp.where(upper, total, delta)
        for offset in range(1, chips):
            log_copy(offset).start()
        group_count = sum(tile[HALF_HEADS : HALF_HEADS + 1, 0:1] for tile in tiles)
        count_out[0] = jnp.broadcast_to(group_count, (8, LANES))
        for k, device in enumerate(peers_x):
            count_copy(0, k, device).start()

    def gather_logs():
        for offset in range(1, chips):
            log_copy(offset).wait_recv()
        for slot in range(slots):
            own = log_out[...] if slot == 0 else log_in[slot]
            far = log_in[chips - slot if slot else slots]
            info = jnp.where(lane < block, own, pltpu.roll(far, block, 1))
            row_info[slot] = jnp.where(lane < 2 * block, info, 0.0)
        total = count_out[0]
        for k, device in enumerate(peers_x):
            count_copy(0, k, device).wait_recv()
            total = total + count_in[0, k]
        count_out[1] = total
        for k, device in enumerate(peers_y):
            count_copy(1, k, device).start()

    def grad_slot(slot):
        for head in range(HALF_HEADS):
            columns = slice(head * HEAD_SIZE, (head + 1) * HEAD_SIZE)
            here = slice(slot * LANES, (slot + 1) * LANES)
            dprob = nt(vx[:, columns], mb[here, columns])
            p = jnp.exp(scores[slot, head] - row_info[slot, head : head + 1])
            ds = p * (dprob - row_info[slot, HALF_HEADS + head : HALF_HEADS + head + 1])
            ds = ds.astype(jnp.bfloat16)
            probs[head, :, here] = p.astype(jnp.bfloat16)
            dscores[head, :, here] = ds
            dq_part[here, columns] = tn(ds, kx[:, columns])

    for hop in range(slots + LAG):
        if hop < slots:
            forward(0, hop)
        if hop == LAG - 1:
            for chunk in range(CHUNKS):
                for way in range(2):
                    if chunk in chunks_of_hop(way, 0, slots - 1):
                        gathered(1, way, 0, chunk).start()
        if LAG <= hop < slots + LAG - 1:
            forward(1, hop - LAG)
        if hop < slots:
            score_slot((hop + 1) % slots)
        if hop == slots:
            combine_logs()
    kv_sent[1].wait_recv()
    gather_logs()
    forward(1, slots - 1)

    def part_for(way, slot, chunk):
        side = slot * LANES + (0 if way and slot else block)
        return dq_part[side : side + block, chunk * wide : (chunk + 1) * wide]

    grad_slot(0)
    for way in range(2):
        for chunk in chunks_of_hop(way, 0, 0):
            rs_out[way, 0, :, chunk * wide : (chunk + 1) * wide] = part_for(way, 0, chunk).astype(jnp.bfloat16)
            scattered(way, 0, chunk).start()
    for hop in range(slots - 1):
        slot = slots - 1 - hop
        grad_slot(slot)
        for chunk in range(CHUNKS):
            columns = slice(chunk * wide, (chunk + 1) * wide)
            for way in range(2):
                part = part_for(way, slot, chunk)
                if chunk in chunks_of_hop(way, hop, 0):
                    scattered(way, hop, chunk).wait_recv()
                    part = part + rs_in[way, hop, :, columns].astype(jnp.float32)
                rs_out[way, hop + 1, :, columns] = part.astype(jnp.bfloat16)
                scattered(way, hop + 1, chunk).start()

    total = count_out[1]
    for k, device in enumerate(peers_y):
        count_copy(1, k, device).wait_recv()
        total = total + count_in[1, k]
    factor = jnp.float32(dp_x * dp_y * chips * block) / total[0:1, 0:1]
    small_factor = factor * HEAD_SIZE ** (-0.5)

    for head in range(HALF_HEADS):
        columns = slice(head * HEAD_SIZE, (head + 1) * HEAD_SIZE)
        grads[1, :, columns] = (nn(probs[head], mb[:, columns]) * factor).astype(jnp.bfloat16)
        for copy in grad_copies(1, head):
            copy.start()
        grads[0, :, columns] = (nn(dscores[head], qb[:, columns]) * small_factor).astype(jnp.bfloat16)
        for copy in grad_copies(0, head):
            copy.start()

    for chunk in range(CHUNKS):
        columns = slice(chunk * wide, (chunk + 1) * wide)
        total = dq_part[0:block, columns]
        for way in range(2):
            scattered(way, slots - 1, chunk).wait_recv()
            total = total + rs_in[way, slots - 1, :, columns].astype(jnp.float32)
        fin[:, columns] = total * small_factor
    my_rows = pl.ds(pl.multiple_of(core * rows, 8), rows)
    their_rows = pl.ds(pl.multiple_of((1 - core) * rows, 8), rows)
    last = remote(fin.at[their_rows], fin_in, fin_send, fin_recv, sibling)
    last.start()
    dq_ref[:, mine] = fin[my_rows, :].astype(jnp.bfloat16)

    for copy in (*staged, count_swap, *kv_sent):
        copy.wait_send()
    for which in range(2):
        for hop in range(slots):
            for way in range(2):
                for chunk in chunks_of_hop(way, hop, slots - 1):
                    gathered(which, way, hop, chunk).wait_send()
    for hop in range(slots):
        for way in range(2):
            for chunk in chunks_of_hop(way, hop, 0):
                scattered(way, hop, chunk).wait_send()
    for slot in range(slots):
        for copy in tile_copies(slot):
            copy.wait_send()
    for offset in range(1, chips):
        log_copy(offset).wait_send()
    for phase, peers in enumerate((peers_x, peers_y)):
        for k, device in enumerate(peers):
            count_copy(phase, k, device).wait_send()
    for which in range(2):
        for head in range(HALF_HEADS):
            near, far = grad_copies(which, head)
            near.wait()
            far.wait()
    last.wait()
    dq_ref[:, theirs] = fin_in[...].astype(jnp.bfloat16)


def local(dp_count, queries, keys, values, attn_out, out_grad, loss_mask, input_lengths, target_lengths):
    rows, features = queries.shape[1:]
    keys_dev = keys.shape[1]
    chips = lax.axis_size("seq") // 2
    slots = chips // 2
    block = 2 * rows
    dp_x, dp_y = (4, 4) if dp_count == 16 else (1, dp_count)
    bf16, f32 = jnp.bfloat16, jnp.float32
    vmem = pl.BlockSpec(memory_space=pltpu.VMEM)
    smem = pl.BlockSpec(memory_space=pltpu.SMEM)
    anywhere = pl.BlockSpec(memory_space=pl.ANY)
    dma = pltpu.SemaphoreType.DMA
    total = chips * block * chips * 2 * keys_dev // chips * HALF
    dq, dk, dv = pl.pallas_call(
        functools.partial(kernel, dp_x, dp_y, chips),
        out_shape=(
            jax.ShapeDtypeStruct((rows, features), bf16),
            jax.ShapeDtypeStruct((keys_dev, features), bf16),
            jax.ShapeDtypeStruct((keys_dev, features), bf16),
        ),
        in_specs=[smem, smem, vmem, vmem, vmem, vmem, anywhere, anywhere],
        out_specs=(vmem, anywhere, anywhere),
        scratch_shapes=[
            pltpu.VMEM((3, rows, HALF), f32),
            pltpu.VMEM((3, rows, HALF), f32),
            pltpu.VMEM((2 * keys_dev, HALF), bf16),
            pltpu.VMEM((2 * keys_dev, HALF), bf16),
            pltpu.VMEM((slots * LANES, HALF), bf16),
            pltpu.VMEM((slots * LANES, HALF), bf16),
            pltpu.VMEM((2 * keys_dev, LANES), jnp.int32),
            pltpu.VMEM((slots, HALF_HEADS, 2 * keys_dev, LANES), f32),
            pltpu.VMEM((HALF_HEADS, 2 * keys_dev, slots * LANES), bf16),
            pltpu.VMEM((HALF_HEADS, 2 * keys_dev, slots * LANES), bf16),
            pltpu.VMEM((slots * LANES, HALF), f32),
            pltpu.VMEM((2, slots, block, HALF), bf16),
            pltpu.VMEM((2, slots, block, HALF), bf16),
            pltpu.VMEM((2, 2 * keys_dev, HALF), bf16),
            pltpu.VMEM((block, HALF), f32),
            pltpu.VMEM((rows, HALF), f32),
            pltpu.VMEM((slots, 8, LANES), f32),
            pltpu.VMEM((chips, 8, LANES), f32),
            pltpu.VMEM((8, LANES), f32),
            pltpu.VMEM((chips, 8, LANES), f32),
            pltpu.VMEM((slots, 8, LANES), f32),
            pltpu.VMEM((3, 8, LANES), f32),
            pltpu.VMEM((3, 3, 8, LANES), f32),
            dma((2,)),
            dma((2,)),
            dma((2,)),
            dma((4,)),
            dma((4,)),
            dma((2, 2, slots, CHUNKS)),
            dma((2, 2, slots, CHUNKS)),
            dma((2, slots, CHUNKS)),
            dma((2, slots, CHUNKS)),
            dma((chips,)),
            dma((chips,)),
            dma((chips,)),
            dma((chips,)),
            dma((2, 3)),
            dma((2, 3)),
            dma((2, HALF_HEADS)),
            dma((2, HALF_HEADS)),
            dma((2, HALF_HEADS)),
            dma,
            dma,
        ],
        compiler_params=pltpu.CompilerParams(
            collective_id=0, has_side_effects=True, vmem_limit_bytes=56 * 1024 * 1024
        ),
        cost_estimate=pl.CostEstimate(flops=10 * total, bytes_accessed=6 * 1024 * 1024, transcendentals=0),
    )(
        input_lengths[0, 0],
        target_lengths[0, 0],
        queries[0],
        out_grad[0],
        attn_out[0],
        loss_mask,
        keys[0],
        values[0],
    )
    return dq[None], dk[None], dv[None]


def solution(mesh):
    return jax.shard_map(
        functools.partial(local, mesh.shape["dp"]),
        mesh=mesh,
        in_specs=(
            P("dp", "seq", None),
            P("dp", "seq", None),
            P("dp", "seq", None),
            P("dp", "seq", None),
            P("dp", "seq", None),
            P("dp", "seq"),
            P("dp", None, None),
            P("dp", None, None),
        ),
        out_specs=(P("dp", "seq", None), P("dp", "seq", None), P("dp", "seq", None)),
        check_vma=False,
    )
```

```python
import functools

import jax
import jax.numpy as jnp
from jax import lax
from jax.experimental import pallas as pl
from jax.experimental.pallas import tpu as pltpu
from jax.sharding import PartitionSpec as P

HEADS = 8
HEAD_SIZE = 256
HALF_HEADS = HEADS // 2
HALF = HALF_HEADS * HEAD_SIZE
LANES = 128
CHUNKS = 2
NEAR = 3
NEVER = -1e30
MESH = pl.DeviceIdType.MESH


def nt(a, b):
    return lax.dot_general(a, b, (((1,), (1,)), ((), ())), preferred_element_type=jnp.float32)


def tn(a, b):
    return lax.dot_general(a, b, (((0,), (0,)), ((), ())), preferred_element_type=jnp.float32)


def nn(a, b):
    return jnp.dot(a, b, preferred_element_type=jnp.float32)


def kernel(
    dp_x,
    dp_y,
    chips,
    in_len,
    out_len,
    q_ref,
    g_ref,
    a_ref,
    mask_ref,
    k_ref,
    v_ref,
    dq_ref,
    dk_ref,
    dv_ref,
    stage_out,
    stage_in,
    kx,
    vx,
    qb,
    mb,
    kdoc,
    near_probs,
    near_dscores,
    probs,
    dscores,
    dq_part,
    rs_in,
    rs_out,
    grads,
    fin,
    fin_in,
    tile_out,
    tile_in,
    log_out,
    log_in,
    delta_ring,
    ell_out,
    ell_in,
    weights,
    count_out,
    count_in,
    kv_local,
    kv_send,
    kv_recv,
    stage_send,
    stage_recv,
    ag_send,
    ag_recv,
    rs_send,
    rs_recv,
    tile_send,
    tile_recv,
    log_send,
    log_recv,
    delta_send,
    delta_recv,
    ell_send,
    ell_recv,
    count_send,
    count_recv,
    out_local,
    out_send,
    out_recv,
    fin_send,
    fin_recv,
):
    rows = q_ref.shape[0]
    keys_dev = k_ref.shape[0]
    block = 2 * rows
    keys_chip = 2 * keys_dev
    slots = chips // 2
    wide = HALF // CHUNKS
    dp = lax.axis_index("dp")
    seq = lax.axis_index("seq")
    z = seq // 2
    core = seq % 2
    sibling = (dp, z * 2 + 1 - core)

    def chip_at(offset):
        return (dp, ((z + offset + chips) % chips) * 2 + core)

    ahead = (chip_at(1), chip_at(-1))
    peers_x = [((dp + dp_y * k) % (dp_x * dp_y), seq) for k in range(1, dp_x)]
    peers_y = [((dp // dp_y) * dp_y + (dp % dp_y + k) % dp_y, seq) for k in range(1, dp_y)]

    mine = pl.ds(pl.multiple_of(core * HALF, HALF), HALF)
    theirs = pl.ds(pl.multiple_of((1 - core) * HALF, HALF), HALF)
    my_keys = pl.ds(pl.multiple_of(core * keys_dev, keys_dev), keys_dev)
    their_keys = pl.ds(pl.multiple_of((1 - core) * keys_dev, keys_dev), keys_dev)

    def remote(src, dst, send, recv, device):
        return pltpu.make_async_remote_copy(
            src_ref=src, dst_ref=dst, send_sem=send, recv_sem=recv, device_id=device, device_id_type=MESH
        )

    kv_own = [
        pltpu.make_async_copy(ref.at[:, mine], buf.at[my_keys], kv_local.at[i])
        for i, (ref, buf) in enumerate(((k_ref, kx), (v_ref, vx)))
    ]
    kv_sent = [
        remote(ref.at[:, theirs], buf.at[my_keys], kv_send.at[i], kv_recv.at[i], sibling)
        for i, (ref, buf) in enumerate(((k_ref, kx), (v_ref, vx)))
    ]
    staged = [
        remote(stage_out.at[i], stage_in.at[i], stage_send.at[i], stage_recv.at[i], sibling) for i in range(3)
    ]
    count_swap = remote(count_out.at[2], count_in.at[2, 0], stage_send.at[3], stage_recv.at[3], sibling)

    def gathered(which, way, hop, chunk):
        buf = (qb, mb)[which]
        source = hop * LANES + (way * block if hop else 0)
        target = block if hop == slots - 1 else (hop + 1) * LANES + way * block
        columns = pl.ds(chunk * wide, wide)
        return remote(
            buf.at[pl.ds(source, block), columns],
            buf.at[pl.ds(target, block), columns],
            ag_send.at[which, way, hop, chunk],
            ag_recv.at[which, way, hop, chunk],
            ahead[way],
        )

    def chunks_of_hop(way, hop, last):
        if hop != last:
            return range(CHUNKS)
        return range(CHUNKS // 2) if way == 0 else range(CHUNKS // 2, CHUNKS)

    def delta_copy(way, hop):
        return remote(
            delta_ring.at[way, hop],
            delta_ring.at[way, hop + 1],
            delta_send.at[way, hop],
            delta_recv.at[way, hop],
            ahead[way],
        )

    def delta_ways(hop):
        return range(2) if hop + 1 < slots else range(1)

    leap = slots - 1 - NEAR

    def scatter_target(way, hop):
        if hop == leap:
            return chip_at(-(NEAR + 1) if way else NEAR + 1)
        return ahead[way]

    def ell_copy(way, hop):
        return remote(
            ell_out.at[way, hop],
            ell_in.at[way, hop],
            ell_send.at[way, hop],
            ell_recv.at[way, hop],
            scatter_target(way, hop),
        )

    def forward(which, hop):
        for way in delta_ways(hop) if which else ():
            delta_copy(way, hop).wait_recv()
            if hop + 1 < slots and way in delta_ways(hop + 1):
                delta_copy(way, hop + 1).start()
        for chunk in range(CHUNKS):
            for way in range(2):
                if chunk in chunks_of_hop(way, hop, slots - 1):
                    gathered(which, way, hop, chunk).wait_recv()
                    if hop + 1 < slots and chunk in chunks_of_hop(way, hop + 1, slots - 1):
                        gathered(which, way, hop + 1, chunk).start()

    def scattered(way, hop, chunk):
        columns = pl.ds(chunk * wide, wide)
        return remote(
            rs_out.at[way, hop, :, columns],
            rs_in.at[way, hop, :, columns],
            rs_send.at[way, hop, chunk],
            rs_recv.at[way, hop, chunk],
            scatter_target(way, hop),
        )

    def tile_copies(slot):
        if slot == 0:
            return [remote(tile_out.at[0], tile_in.at[slots], tile_send.at[slots], tile_recv.at[slots], chip_at(slots))]
        return [
            remote(tile_out.at[slot], tile_in.at[slot], tile_send.at[slot], tile_recv.at[slot], chip_at(-slot)),
            remote(
                tile_out.at[slot],
                tile_in.at[slots + slot],
                tile_send.at[slots + slot],
                tile_recv.at[slots + slot],
                chip_at(slot),
            ),
        ]

    def log_copy(offset):
        return remote(log_out, log_in.at[offset], log_send.at[offset], log_recv.at[offset], chip_at(offset))

    def count_copy(phase, k, device):
        return remote(
            count_out.at[phase], count_in.at[phase, k], count_send.at[phase, k], count_recv.at[phase, k], device
        )

    def grad_copies(which, head):
        out = (dk_ref, dv_ref)[which]
        columns = pl.ds(head * HEAD_SIZE, HEAD_SIZE)
        target = pl.ds(pl.multiple_of(core * HALF + head * HEAD_SIZE, HEAD_SIZE), HEAD_SIZE)
        return [
            pltpu.make_async_copy(
                grads.at[which, my_keys, columns], out.at[:, target], out_local.at[which, head]
            ),
            remote(
                grads.at[which, their_keys, columns],
                out.at[:, target],
                out_send.at[which, head],
                out_recv.at[which, head],
                sibling,
            ),
        ]

    for copy in kv_own:
        copy.start()
    barrier = pltpu.get_barrier_semaphore()
    greeted = [sibling, *ahead, *peers_x, *peers_y]
    for device in greeted:
        pl.semaphore_signal(barrier, inc=1, device_id=device, device_id_type=MESH)

    mask_row = mask_ref[...]
    eye = lax.broadcasted_iota(jnp.int32, (rows, rows), 0) == lax.broadcasted_iota(jnp.int32, (rows, rows), 1)
    mask_column = jnp.sum(jnp.where(eye, mask_row, 0), axis=1, keepdims=True).astype(jnp.float32)
    count_out[2] = jnp.full((8, LANES), jnp.sum(mask_row).astype(jnp.float32))
    stage_out[0] = q_ref[:, theirs].astype(jnp.float32)
    pl.semaphore_wait(barrier, len(greeted))
    staged[0].start()
    stage_out[1] = g_ref[:, theirs].astype(jnp.float32) * mask_column
    staged[1].start()
    stage_out[2] = a_ref[:, theirs].astype(jnp.float32)
    staged[2].start()
    count_swap.start()
    for copy in kv_sent:
        copy.start()

    def both(own, other):
        return jnp.concatenate([jnp.where(core == 0, own, other), jnp.where(core == 0, other, own)], axis=0)

    staged[0].wait_recv()
    qb[0:block, :] = both(q_ref[:, mine].astype(jnp.float32), stage_in[0]).astype(jnp.bfloat16)
    for chunk in range(CHUNKS):
        for way in range(2):
            gathered(0, way, 0, chunk).start()
    staged[1].wait_recv()
    masked = both(g_ref[:, mine].astype(jnp.float32) * mask_column, stage_in[1])
    mb[0:block, :] = masked.astype(jnp.bfloat16)
    for chunk in range(CHUNKS):
        for way in range(2):
            gathered(1, way, 0, chunk).start()

    staged[2].wait_recv()
    product = masked * both(a_ref[:, mine].astype(jnp.float32), stage_in[2])
    product = jnp.concatenate([product, jnp.zeros((LANES - block, HALF), jnp.float32)], axis=0)
    high = product.astype(jnp.bfloat16)
    low = (product - high.astype(jnp.float32)).astype(jnp.bfloat16)
    head_of = lax.broadcasted_iota(jnp.int32, (8, HALF), 1) // HEAD_SIZE
    picks = (head_of == lax.broadcasted_iota(jnp.int32, (8, HALF), 0)).astype(jnp.bfloat16)
    delta = (nt(picks, high) + nt(picks, low)).astype(jnp.bfloat16).astype(jnp.float32)[:HALF_HEADS]
    for way in range(2):
        delta_ring[way, 0] = delta
        delta_copy(way, 0).start()

    for slot in range(slots):
        for buf in (qb, mb):
            buf[slot * LANES + 2 * block : (slot + 1) * LANES, :] = jnp.zeros(
                (LANES - 2 * block, HALF), jnp.bfloat16
            )

    ends = [in_len[0]]
    row_ends = [out_len[0]]
    for d in range(1, 3):
        ends.append(ends[-1] + in_len[d])
        row_ends.append(row_ends[-1] + out_len[d])
    key_at = z * keys_chip + lax.broadcasted_iota(jnp.int32, (keys_chip, LANES), 0)
    kdoc[...] = sum((key_at >= end).astype(jnp.int32) for end in ends)
    lane = lax.broadcasted_iota(jnp.int32, (1, LANES), 1)
    opening = lax.broadcasted_iota(jnp.int32, (HALF_HEADS, LANES), 0) < HALF_HEADS // 2

    count_swap.wait_recv()
    chip_count = count_out[2] + count_in[2, 0]

    def score_slot(slot):
        left = (z - slot + chips) % chips
        right = (z + (slot if slot else slots)) % chips
        at = jnp.where(lane < block, left * block + lane, right * block + lane - block)
        doc = sum((at >= end).astype(jnp.int32) for end in row_ends)
        doc = jnp.where(lane < 2 * block, doc, -1)
        for head in range(HALF_HEADS):
            columns = slice(head * HEAD_SIZE, (head + 1) * HEAD_SIZE)
            s = nt(kx[:, columns], qb[slot * LANES : (slot + 1) * LANES, columns]) * HEAD_SIZE ** (-0.5)
            s = jnp.where(kdoc[...] == doc, s, NEVER)
            top = jnp.max(s, axis=0, keepdims=True)
            e = jnp.exp(s - top)
            total = jnp.sum(e, axis=0, keepdims=True)
            near_probs[slot, head] = e * (1.0 / total)
            ell = top + jnp.log(total)
            tile_out[slot, head : head + 1] = jnp.where(lane < 2 * block, ell, chip_count[0:1])
        for copy in tile_copies(slot):
            copy.start()

    def combine_logs():
        for slot in range(slots):
            for copy in tile_copies(slot):
                copy.wait_recv()
        tiles = [tile_out[0]] + [tile_in[i] for i in range(1, slots)]
        tiles += [pltpu.roll(tile_in[i], LANES - block, 1) for i in range(slots, chips)]
        top = functools.reduce(jnp.maximum, tiles)
        log_out[...] = top + jnp.log(sum(jnp.exp(tile - top) for tile in tiles))
        for offset in range(1, chips):
            log_copy(offset).start()
        counts = [tile_out[0]] + [tile_in[i] for i in range(1, chips)]
        group_count = sum(tile[0:1, LANES - 1 : LANES] for tile in counts)
        count_out[0] = jnp.broadcast_to(group_count, (8, LANES))
        for k, device in enumerate(peers_x):
            count_copy(0, k, device).start()

    def gather_logs():
        for offset in range(1, chips):
            log_copy(offset).wait_recv()

    def pass_count():
        total = count_out[0]
        for k, device in enumerate(peers_x):
            count_copy(0, k, device).wait_recv()
            total = total + count_in[0, k]
        count_out[1] = total
        for k, device in enumerate(peers_y):
            count_copy(1, k, device).start()

    def finish_count():
        total = count_out[1]
        for k, device in enumerate(peers_y):
            count_copy(1, k, device).wait_recv()
            total = total + count_in[1, k]
        return jnp.float32(dp_x * dp_y * chips * block) / total[0:1, 0:1]

    def grad_slot(slot):
        far = delta_ring[1, slot] if slot else delta_ring[0, slots]
        deltas = jnp.where(lane < block, delta_ring[0, slot], pltpu.roll(far, block, 1))
        here = slice(slot * LANES, (slot + 1) * LANES)
        for head in range(HALF_HEADS):
            columns = slice(head * HEAD_SIZE, (head + 1) * HEAD_SIZE)
            dprob = nt(vx[:, columns], mb[here, columns])
            ds = near_probs[slot, head] * (dprob - deltas[head : head + 1])
            near_dscores[slot, head] = ds
            dq_part[here, columns] = tn(ds.astype(jnp.bfloat16), kx[:, columns])

    def grad_head(head, factor):
        columns = slice(head * HEAD_SIZE, (head + 1) * HEAD_SIZE)
        for slot in range(slots):
            here = slice(slot * LANES, (slot + 1) * LANES)
            own = log_out[...] if slot == 0 else log_in[slot]
            far = pltpu.roll(log_in[chips - slot if slot else slots], block, 1)
            full = jnp.where(lane < block, own, far)[head : head + 1]
            scale = jnp.where(lane < 2 * block, jnp.exp(tile_out[slot, head : head + 1] - full), 0.0)
            probs[:, here] = (near_probs[slot, head] * scale).astype(jnp.bfloat16)
            dscores[:, here] = (near_dscores[slot, head] * scale).astype(jnp.bfloat16)
        grads[1, :, columns] = (nn(probs[...], mb[:, columns]) * factor).astype(jnp.bfloat16)
        for copy in grad_copies(1, head):
            copy.start()
        small_factor = factor * HEAD_SIZE ** (-0.5)
        grads[0, :, columns] = (nn(dscores[...], qb[:, columns]) * small_factor).astype(jnp.bfloat16)
        for copy in grad_copies(0, head):
            copy.start()

    for hop in range(slots):
        slot = (hop + 1) % slots
        forward(0, hop)
        if hop == 0:
            kv_own[0].wait()
            kv_sent[0].wait_recv()
        score_slot(slot)
        forward(1, hop)
        if hop == 0:
            kv_own[1].wait()
            kv_sent[1].wait_recv()
        grad_slot(slot)
    ell_out[0, 0] = jnp.where(opening, tile_out[0], NEVER)
    ell_out[1, 0] = jnp.where(opening, NEVER, pltpu.roll(tile_out[0], LANES - block, 1))
    for way in range(2):
        ell_copy(way, 0).start()

    def part_for(way, slot, columns):
        side = slot * LANES + (0 if way and slot else block)
        return dq_part[side : side + block, columns]

    def chunk_columns(chunk):
        return slice(chunk * wide, (chunk + 1) * wide)

    for way in range(2):
        for chunk in chunks_of_hop(way, 0, 0):
            columns = chunk_columns(chunk)
            rs_out[way, 0, :, columns] = part_for(way, 0, columns).astype(jnp.bfloat16)
            scattered(way, 0, chunk).start()

    def scatter_step(hop):
        slot = slots - 1 - hop
        here = tile_out[slot]
        if hop == leap:
            after = here
        else:
            for way in range(2):
                ell_copy(way, hop).wait_recv()
            before = jnp.where(lane < block, ell_in[1, hop], ell_in[0, hop])
            top = jnp.maximum(before, here)
            after = top + jnp.log(jnp.exp(before - top) + jnp.exp(here - top))
            weights[...] = jnp.concatenate([jnp.exp(before - after), jnp.exp(here - after)], axis=0).T
        for way in range(2):
            ell_out[way, hop + 1] = after
            ell_copy(way, hop + 1).start()
        for chunk in range(CHUNKS):
            for way in range(2):
                arrives = hop != leap and chunk in chunks_of_hop(way, hop, 0)
                if arrives:
                    scattered(way, hop, chunk).wait_recv()
                side = slice(0, block) if way else slice(block, 2 * block)
                for head in range(chunk * wide // HEAD_SIZE, (chunk + 1) * wide // HEAD_SIZE):
                    columns = slice(head * HEAD_SIZE, (head + 1) * HEAD_SIZE)
                    part = part_for(way, slot, columns)
                    if hop != leap:
                        part *= weights[side, HALF_HEADS + head : HALF_HEADS + head + 1]
                    if arrives:
                        part += rs_in[way, hop, :, columns].astype(jnp.float32) * weights[side, head : head + 1]
                    rs_out[way, hop + 1, :, columns] = part.astype(jnp.bfloat16)
                scattered(way, hop + 1, chunk).start()

    scatter_step(leap)
    for step in range(leap):
        scatter_step(step)
        if leap + 1 + step < slots - 1:
            scatter_step(leap + 1 + step)
        if step == min(1, leap - 1):
            combine_logs()
        if step == min(2, leap - 1):
            pass_count()
    gather_logs()
    factor = finish_count()
    for head in range(HALF_HEADS):
        grad_head(head, factor)

    for way in range(2):
        for hop in (leap, slots - 1):
            ell_copy(way, hop).wait_recv()
    sums = [(way, hop) for hop in (slots - 1, leap) for way in range(2)]
    tiles = [ell_in[way, hop] if way else pltpu.roll(ell_in[way, hop], LANES - block, 1) for way, hop in sums]
    scales = [jnp.exp(jnp.minimum(tile - log_out[...], 0.0)) for tile in (*tiles, tile_out[0], tile_out[0])]
    columns_of = [jnp.concatenate(scales[i : i + 2], axis=0).T for i in range(0, 6, 2)]
    small_factor = factor * HEAD_SIZE ** (-0.5)
    for chunk in range(CHUNKS):
        for way, hop in sums:
            scattered(way, hop, chunk).wait_recv()
        for head in range(chunk * wide // HEAD_SIZE, (chunk + 1) * wide // HEAD_SIZE):
            columns = slice(head * HEAD_SIZE, (head + 1) * HEAD_SIZE)
            total = dq_part[0:block, columns] * columns_of[2][:block, head : head + 1]
            for i, (way, hop) in enumerate(sums):
                part = rs_in[way, hop, :, columns].astype(jnp.float32)
                at = i % 2 * HALF_HEADS + head
                total += part * columns_of[i // 2][:block, at : at + 1]
            fin[:, columns] = total * small_factor
    my_rows = pl.ds(pl.multiple_of(core * rows, 8), rows)
    their_rows = pl.ds(pl.multiple_of((1 - core) * rows, 8), rows)
    last = remote(fin.at[their_rows], fin_in, fin_send, fin_recv, sibling)
    last.start()
    dq_ref[:, mine] = fin[my_rows, :].astype(jnp.bfloat16)

    for copy in (*staged, count_swap, *kv_sent):
        copy.wait_send()
    for which in range(2):
        for hop in range(slots):
            for way in range(2):
                for chunk in chunks_of_hop(way, hop, slots - 1):
                    gathered(which, way, hop, chunk).wait_send()
    for hop in range(slots):
        for way in range(2):
            for chunk in chunks_of_hop(way, hop, 0):
                scattered(way, hop, chunk).wait_send()
    for hop in range(slots):
        for way in range(2):
            ell_copy(way, hop).wait_send()
        for way in delta_ways(hop):
            delta_copy(way, hop).wait_send()
    for slot in range(slots):
        for copy in tile_copies(slot):
            copy.wait_send()
    for offset in range(1, chips):
        log_copy(offset).wait_send()
    for phase, peers in enumerate((peers_x, peers_y)):
        for k, device in enumerate(peers):
            count_copy(phase, k, device).wait_send()
    for which in range(2):
        for head in range(HALF_HEADS):
            near, far = grad_copies(which, head)
            near.wait()
            far.wait()
    last.wait()
    dq_ref[:, theirs] = fin_in[...].astype(jnp.bfloat16)


def hand_over(*refs):
    sources, targets, held = refs[:3], refs[3:6], refs[6:9]
    in_sems, out_sems = refs[9:]
    pieces = []
    for source, target, buf in zip(sources, targets, held):
        parts = 4 if source.shape[0] % 64 == 0 else 1
        size = source.shape[0] // parts
        for part in range(parts):
            rows = pl.ds(part * size, size)
            i = len(pieces)
            pieces.append(
                (
                    pltpu.make_async_copy(source.at[rows], buf.at[rows], in_sems.at[i]),
                    pltpu.make_async_copy(buf.at[rows], target.at[rows], out_sems.at[i]),
                )
            )
    for fetch, _ in pieces:
        fetch.start()
    for fetch, store in pieces:
        fetch.wait()
        store.start()
    for _, store in pieces:
        store.wait()


def local(dp_count, queries, keys, values, attn_out, out_grad, loss_mask, input_lengths, target_lengths):
    rows, features = queries.shape[1:]
    keys_dev = keys.shape[1]
    chips = lax.axis_size("seq") // 2
    slots = chips // 2
    block = 2 * rows
    dp_x, dp_y = (4, 4) if dp_count == 16 else (1, dp_count)
    bf16, f32 = jnp.bfloat16, jnp.float32
    vmem = pl.BlockSpec(memory_space=pltpu.VMEM)
    smem = pl.BlockSpec(memory_space=pltpu.SMEM)
    anywhere = pl.BlockSpec(memory_space=pl.ANY)
    dma = pltpu.SemaphoreType.DMA
    total = chips * block * chips * 2 * keys_dev // chips * HALF
    dq, dk, dv = pl.pallas_call(
        functools.partial(kernel, dp_x, dp_y, chips),
        out_shape=(
            jax.ShapeDtypeStruct((rows, features), bf16),
            jax.ShapeDtypeStruct((keys_dev, features), bf16),
            jax.ShapeDtypeStruct((keys_dev, features), bf16),
        ),
        in_specs=[smem, smem, vmem, vmem, vmem, vmem, anywhere, anywhere],
        out_specs=(vmem, anywhere, anywhere),
        scratch_shapes=[
            pltpu.VMEM((3, rows, HALF), f32),
            pltpu.VMEM((3, rows, HALF), f32),
            pltpu.VMEM((2 * keys_dev, HALF), bf16),
            pltpu.VMEM((2 * keys_dev, HALF), bf16),
            pltpu.VMEM((slots * LANES, HALF), bf16),
            pltpu.VMEM((slots * LANES, HALF), bf16),
            pltpu.VMEM((2 * keys_dev, LANES), jnp.int32),
            pltpu.VMEM((slots, HALF_HEADS, 2 * keys_dev, LANES), f32),
            pltpu.VMEM((slots, HALF_HEADS, 2 * keys_dev, LANES), f32),
            pltpu.VMEM((2 * keys_dev, slots * LANES), bf16),
            pltpu.VMEM((2 * keys_dev, slots * LANES), bf16),
            pltpu.VMEM((slots * LANES, HALF), f32),
            pltpu.VMEM((2, slots, block, HALF), bf16),
            pltpu.VMEM((2, slots, block, HALF), bf16),
            pltpu.VMEM((2, 2 * keys_dev, HALF), bf16),
            pltpu.VMEM((block, HALF), f32),
            pltpu.VMEM((rows, HALF), f32),
            pltpu.VMEM((slots, HALF_HEADS, LANES), f32),
            pltpu.VMEM((chips, HALF_HEADS, LANES), f32),
            pltpu.VMEM((HALF_HEADS, LANES), f32),
            pltpu.VMEM((chips, HALF_HEADS, LANES), f32),
            pltpu.VMEM((2, slots + 1, HALF_HEADS, LANES), f32),
            pltpu.VMEM((2, slots, HALF_HEADS, LANES), f32),
            pltpu.VMEM((2, slots, HALF_HEADS, LANES), f32),
            pltpu.VMEM((LANES, 2 * HALF_HEADS), f32),
            pltpu.VMEM((3, 8, LANES), f32),
            pltpu.VMEM((3, 3, 8, LANES), f32),
            dma((2,)),
            dma((2,)),
            dma((2,)),
            dma((4,)),
            dma((4,)),
            dma((2, 2, slots, CHUNKS)),
            dma((2, 2, slots, CHUNKS)),
            dma((2, slots, CHUNKS)),
            dma((2, slots, CHUNKS)),
            dma((chips,)),
            dma((chips,)),
            dma((chips,)),
            dma((chips,)),
            dma((2, slots)),
            dma((2, slots)),
            dma((2, slots)),
            dma((2, slots)),
            dma((2, 3)),
            dma((2, 3)),
            dma((2, HALF_HEADS)),
            dma((2, HALF_HEADS)),
            dma((2, HALF_HEADS)),
            dma,
            dma,
        ],
        compiler_params=pltpu.CompilerParams(
            collective_id=0, has_side_effects=True, vmem_limit_bytes=56 * 1024 * 1024
        ),
        cost_estimate=pl.CostEstimate(flops=10 * total, bytes_accessed=6 * 1024 * 1024, transcendentals=0),
    )(
        input_lengths[0, 0],
        target_lengths[0, 0],
        queries[0],
        out_grad[0],
        attn_out[0],
        loss_mask,
        keys[0],
        values[0],
    )
    results = (dk, dv, dq)
    dk, dv, dq = pl.pallas_call(
        hand_over,
        out_shape=tuple(jax.ShapeDtypeStruct(array.shape, array.dtype) for array in results),
        in_specs=[anywhere] * 3,
        out_specs=(anywhere,) * 3,
        scratch_shapes=[*(pltpu.VMEM(array.shape, array.dtype) for array in results), dma((9,)), dma((9,))],
        compiler_params=pltpu.CompilerParams(vmem_limit_bytes=56 * 1024 * 1024),
        cost_estimate=pl.CostEstimate(flops=0, bytes_accessed=5 * 1024 * 1024, transcendentals=0),
    )(*results)
    return dq[None], dk[None], dv[None]


def solution(mesh):
    return jax.shard_map(
        functools.partial(local, mesh.shape["dp"]),
        mesh=mesh,
        in_specs=(
            P("dp", "seq", None),
            P("dp", "seq", None),
            P("dp", "seq", None),
            P("dp", "seq", None),
            P("dp", "seq", None),
            P("dp", "seq"),
            P("dp", None, None),
            P("dp", None, None),
        ),
        out_specs=(P("dp", "seq", None), P("dp", "seq", None), P("dp", "seq", None)),
        check_vma=False,
    )
```

```python
import functools

import jax
import jax.numpy as jnp
from jax import lax
from jax.experimental import pallas as pl
from jax.experimental.pallas import tpu as pltpu
from jax.sharding import PartitionSpec as P

HEADS = 8
HEAD_SIZE = 256
HALF_HEADS = HEADS // 2
HALF = HALF_HEADS * HEAD_SIZE
LANES = 128
CHUNKS = 2
NEAR = 3
NEVER = -1e30
MESH = pl.DeviceIdType.MESH


def nt(a, b):
    return lax.dot_general(a, b, (((1,), (1,)), ((), ())), preferred_element_type=jnp.float32)


def tn(a, b):
    return lax.dot_general(a, b, (((0,), (0,)), ((), ())), preferred_element_type=jnp.float32)


def nn(a, b):
    return jnp.dot(a, b, preferred_element_type=jnp.float32)


def kernel(
    dp_x,
    dp_y,
    chips,
    in_len,
    out_len,
    q_ref,
    g_ref,
    a_ref,
    mask_ref,
    k_ref,
    v_ref,
    dq_ref,
    dk_ref,
    dv_ref,
    stage_out,
    stage_in,
    kx,
    vx,
    qb,
    mb,
    kdoc,
    near_probs,
    near_dscores,
    probs,
    dscores,
    dq_part,
    rs_in,
    rs_out,
    grads,
    fin,
    fin_in,
    tile_out,
    tile_in,
    log_out,
    log_in,
    delta_ring,
    ell_out,
    ell_in,
    weights,
    count_out,
    count_in,
    kv_local,
    kv_send,
    kv_recv,
    stage_send,
    stage_recv,
    ag_send,
    ag_recv,
    rs_send,
    rs_recv,
    tile_send,
    tile_recv,
    log_send,
    log_recv,
    delta_send,
    delta_recv,
    ell_send,
    ell_recv,
    count_send,
    count_recv,
    out_local,
    out_send,
    out_recv,
    fin_send,
    fin_recv,
):
    rows = q_ref.shape[0]
    keys_dev = k_ref.shape[0]
    block = 2 * rows
    keys_chip = 2 * keys_dev
    slots = chips // 2
    wide = HALF // CHUNKS
    dp = lax.axis_index("dp")
    seq = lax.axis_index("seq")
    z = seq // 2
    core = seq % 2
    sibling = (dp, z * 2 + 1 - core)

    def chip_at(offset):
        return (dp, ((z + offset + chips) % chips) * 2 + core)

    ahead = (chip_at(1), chip_at(-1))
    peers_x = [((dp + dp_y * k) % (dp_x * dp_y), seq) for k in range(1, dp_x)]
    peers_y = [((dp // dp_y) * dp_y + (dp % dp_y + k) % dp_y, seq) for k in range(1, dp_y)]

    mine = pl.ds(pl.multiple_of(core * HALF, HALF), HALF)
    theirs = pl.ds(pl.multiple_of((1 - core) * HALF, HALF), HALF)
    my_keys = pl.ds(pl.multiple_of(core * keys_dev, keys_dev), keys_dev)
    their_keys = pl.ds(pl.multiple_of((1 - core) * keys_dev, keys_dev), keys_dev)

    def remote(src, dst, send, recv, device):
        return pltpu.make_async_remote_copy(
            src_ref=src, dst_ref=dst, send_sem=send, recv_sem=recv, device_id=device, device_id_type=MESH
        )

    kv_own = [
        pltpu.make_async_copy(ref.at[:, mine], buf.at[my_keys], kv_local.at[i])
        for i, (ref, buf) in enumerate(((k_ref, kx), (v_ref, vx)))
    ]
    kv_sent = [
        remote(ref.at[:, theirs], buf.at[my_keys], kv_send.at[i], kv_recv.at[i], sibling)
        for i, (ref, buf) in enumerate(((k_ref, kx), (v_ref, vx)))
    ]
    staged = [
        remote(stage_out.at[i], stage_in.at[i], stage_send.at[i], stage_recv.at[i], sibling) for i in range(3)
    ]
    count_swap = remote(count_out.at[2], count_in.at[2, 0], stage_send.at[3], stage_recv.at[3], sibling)

    def gathered(which, way, hop, chunk):
        buf = (qb, mb)[which]
        source = hop * LANES + (way * block if hop else 0)
        target = block if hop == slots - 1 else (hop + 1) * LANES + way * block
        columns = pl.ds(chunk * wide, wide)
        return remote(
            buf.at[pl.ds(source, block), columns],
            buf.at[pl.ds(target, block), columns],
            ag_send.at[which, way, hop, chunk],
            ag_recv.at[which, way, hop, chunk],
            ahead[way],
        )

    def chunks_of_hop(way, hop, last):
        if hop != last:
            return range(CHUNKS)
        return range(CHUNKS // 2) if way == 0 else range(CHUNKS // 2, CHUNKS)

    def delta_copy(way, hop):
        return remote(
            delta_ring.at[way, hop],
            delta_ring.at[way, hop + 1],
            delta_send.at[way, hop],
            delta_recv.at[way, hop],
            ahead[way],
        )

    def delta_ways(hop):
        return range(2) if hop + 1 < slots else range(1)

    leap = slots - 1 - NEAR

    def scatter_target(way, hop):
        if hop == leap:
            return chip_at(-(NEAR + 1) if way else NEAR + 1)
        return ahead[way]

    def ell_copy(way, hop):
        return remote(
            ell_out.at[way, hop],
            ell_in.at[way, hop],
            ell_send.at[way, hop],
            ell_recv.at[way, hop],
            scatter_target(way, hop),
        )

    def forward(which, hop):
        for way in delta_ways(hop) if which else ():
            delta_copy(way, hop).wait_recv()
            if hop + 1 < slots and way in delta_ways(hop + 1):
                delta_copy(way, hop + 1).start()
        for chunk in range(CHUNKS):
            for way in range(2):
                if chunk in chunks_of_hop(way, hop, slots - 1):
                    gathered(which, way, hop, chunk).wait_recv()
                    if hop + 1 < slots and chunk in chunks_of_hop(way, hop + 1, slots - 1):
                        gathered(which, way, hop + 1, chunk).start()

    def scattered(way, hop, chunk):
        columns = pl.ds(chunk * wide, wide)
        return remote(
            rs_out.at[way, hop, :, columns],
            rs_in.at[way, hop, :, columns],
            rs_send.at[way, hop, chunk],
            rs_recv.at[way, hop, chunk],
            scatter_target(way, hop),
        )

    def tile_copies(slot):
        if slot == 0:
            return [remote(tile_out.at[0], tile_in.at[slots], tile_send.at[slots], tile_recv.at[slots], chip_at(slots))]
        return [
            remote(tile_out.at[slot], tile_in.at[slot], tile_send.at[slot], tile_recv.at[slot], chip_at(-slot)),
            remote(
                tile_out.at[slot],
                tile_in.at[slots + slot],
                tile_send.at[slots + slot],
                tile_recv.at[slots + slot],
                chip_at(slot),
            ),
        ]

    def log_copy(offset):
        return remote(log_out, log_in.at[offset], log_send.at[offset], log_recv.at[offset], chip_at(offset))

    def count_copy(phase, k, device):
        return remote(
            count_out.at[phase], count_in.at[phase, k], count_send.at[phase, k], count_recv.at[phase, k], device
        )

    def grad_copies(which, head):
        out = (dk_ref, dv_ref)[which]
        columns = pl.ds(head * HEAD_SIZE, HEAD_SIZE)
        target = pl.ds(pl.multiple_of(core * HALF + head * HEAD_SIZE, HEAD_SIZE), HEAD_SIZE)
        return [
            pltpu.make_async_copy(
                grads.at[which, my_keys, columns], out.at[:, target], out_local.at[which, head]
            ),
            remote(
                grads.at[which, their_keys, columns],
                out.at[:, target],
                out_send.at[which, head],
                out_recv.at[which, head],
                sibling,
            ),
        ]

    for copy in kv_own:
        copy.start()
    barrier = pltpu.get_barrier_semaphore()
    greeted = [sibling, *ahead, *peers_x, *peers_y]
    for device in greeted:
        pl.semaphore_signal(barrier, inc=1, device_id=device, device_id_type=MESH)

    mask_row = mask_ref[...]
    eye = lax.broadcasted_iota(jnp.int32, (rows, rows), 0) == lax.broadcasted_iota(jnp.int32, (rows, rows), 1)
    mask_column = jnp.sum(jnp.where(eye, mask_row, 0), axis=1, keepdims=True).astype(jnp.float32)
    count_out[2] = jnp.full((8, LANES), jnp.sum(mask_row).astype(jnp.float32))
    stage_out[0] = q_ref[:, theirs].astype(jnp.float32)
    pl.semaphore_wait(barrier, len(greeted))
    staged[0].start()
    stage_out[1] = g_ref[:, theirs].astype(jnp.float32) * mask_column
    staged[1].start()
    stage_out[2] = a_ref[:, theirs].astype(jnp.float32)
    staged[2].start()
    count_swap.start()

    def both(own, other):
        return jnp.concatenate([jnp.where(core == 0, own, other), jnp.where(core == 0, other, own)], axis=0)

    staged[0].wait_recv()
    qb[0:block, :] = both(q_ref[:, mine].astype(jnp.float32), stage_in[0]).astype(jnp.bfloat16)
    for chunk in range(CHUNKS):
        for way in range(2):
            gathered(0, way, 0, chunk).start()
    staged[1].wait_recv()
    masked = both(g_ref[:, mine].astype(jnp.float32) * mask_column, stage_in[1])
    mb[0:block, :] = masked.astype(jnp.bfloat16)
    for chunk in range(CHUNKS):
        for way in range(2):
            gathered(1, way, 0, chunk).start()
    for copy in kv_sent:
        copy.start()

    staged[2].wait_recv()
    product = masked * both(a_ref[:, mine].astype(jnp.float32), stage_in[2])
    product = jnp.concatenate([product, jnp.zeros((LANES - block, HALF), jnp.float32)], axis=0)
    high = product.astype(jnp.bfloat16)
    low = (product - high.astype(jnp.float32)).astype(jnp.bfloat16)
    head_of = lax.broadcasted_iota(jnp.int32, (8, HALF), 1) // HEAD_SIZE
    picks = (head_of == lax.broadcasted_iota(jnp.int32, (8, HALF), 0)).astype(jnp.bfloat16)
    delta = (nt(picks, high) + nt(picks, low)).astype(jnp.bfloat16).astype(jnp.float32)[:HALF_HEADS]
    for way in range(2):
        delta_ring[way, 0] = delta
        delta_copy(way, 0).start()

    for slot in range(slots):
        for buf in (qb, mb):
            buf[slot * LANES + 2 * block : (slot + 1) * LANES, :] = jnp.zeros(
                (LANES - 2 * block, HALF), jnp.bfloat16
            )

    ends = [in_len[0]]
    row_ends = [out_len[0]]
    for d in range(1, 3):
        ends.append(ends[-1] + in_len[d])
        row_ends.append(row_ends[-1] + out_len[d])
    key_at = z * keys_chip + lax.broadcasted_iota(jnp.int32, (keys_chip, LANES), 0)
    kdoc[...] = sum((key_at >= end).astype(jnp.int32) for end in ends)
    lane = lax.broadcasted_iota(jnp.int32, (1, LANES), 1)
    opening = lax.broadcasted_iota(jnp.int32, (HALF_HEADS, LANES), 0) < HALF_HEADS // 2

    count_swap.wait_recv()
    chip_count = count_out[2] + count_in[2, 0]

    def score_slot(slot):
        left = (z - slot + chips) % chips
        right = (z + (slot if slot else slots)) % chips
        at = jnp.where(lane < block, left * block + lane, right * block + lane - block)
        doc = sum((at >= end).astype(jnp.int32) for end in row_ends)
        doc = jnp.where(lane < 2 * block, doc, -1)
        for head in range(HALF_HEADS):
            columns = slice(head * HEAD_SIZE, (head + 1) * HEAD_SIZE)
            s = nt(kx[:, columns], qb[slot * LANES : (slot + 1) * LANES, columns]) * HEAD_SIZE ** (-0.5)
            s = jnp.where(kdoc[...] == doc, s, NEVER)
            top = jnp.max(s, axis=0, keepdims=True)
            e = jnp.exp(s - top)
            total = jnp.sum(e, axis=0, keepdims=True)
            near_probs[slot, head] = e * (1.0 / total)
            ell = top + jnp.log(total)
            tile_out[slot, head : head + 1] = jnp.where(lane < 2 * block, ell, chip_count[0:1])
        for copy in tile_copies(slot):
            copy.start()

    def combine_logs():
        for slot in range(slots):
            for copy in tile_copies(slot):
                copy.wait_recv()
        tiles = [tile_out[0]] + [tile_in[i] for i in range(1, slots)]
        tiles += [pltpu.roll(tile_in[i], LANES - block, 1) for i in range(slots, chips)]
        top = functools.reduce(jnp.maximum, tiles)
        log_out[...] = top + jnp.log(sum(jnp.exp(tile - top) for tile in tiles))
        for offset in sorted(range(1, chips), key=lambda offset: abs(offset - slots)):
            log_copy(offset).start()
        counts = [tile_out[0]] + [tile_in[i] for i in range(1, chips)]
        group_count = sum(tile[0:1, LANES - 1 : LANES] for tile in counts)
        count_out[0] = jnp.broadcast_to(group_count, (8, LANES))
        for k, device in enumerate(peers_x):
            count_copy(0, k, device).start()

    def gather_logs():
        for offset in range(1, chips):
            log_copy(offset).wait_recv()

    def pass_count():
        total = count_out[0]
        for k, device in enumerate(peers_x):
            count_copy(0, k, device).wait_recv()
            total = total + count_in[0, k]
        count_out[1] = total
        for k, device in enumerate(peers_y):
            count_copy(1, k, device).start()

    def finish_count():
        total = count_out[1]
        for k, device in enumerate(peers_y):
            count_copy(1, k, device).wait_recv()
            total = total + count_in[1, k]
        return jnp.float32(dp_x * dp_y * chips * block) / total[0:1, 0:1]

    def grad_slot(slot):
        far = delta_ring[1, slot] if slot else delta_ring[0, slots]
        deltas = jnp.where(lane < block, delta_ring[0, slot], pltpu.roll(far, block, 1))
        here = slice(slot * LANES, (slot + 1) * LANES)
        for head in range(HALF_HEADS):
            columns = slice(head * HEAD_SIZE, (head + 1) * HEAD_SIZE)
            dprob = nt(vx[:, columns], mb[here, columns])
            ds = near_probs[slot, head] * (dprob - deltas[head : head + 1])
            near_dscores[slot, head] = ds
            dq_part[here, columns] = tn(ds.astype(jnp.bfloat16), kx[:, columns])

    def grad_head(head, factor):
        columns = slice(head * HEAD_SIZE, (head + 1) * HEAD_SIZE)
        for slot in range(slots):
            here = slice(slot * LANES, (slot + 1) * LANES)
            own = log_out[...] if slot == 0 else log_in[slot]
            far = pltpu.roll(log_in[chips - slot if slot else slots], block, 1)
            full = jnp.where(lane < block, own, far)[head : head + 1]
            scale = jnp.where(lane < 2 * block, jnp.exp(tile_out[slot, head : head + 1] - full), 0.0)
            probs[:, here] = (near_probs[slot, head] * scale).astype(jnp.bfloat16)
            dscores[:, here] = (near_dscores[slot, head] * scale).astype(jnp.bfloat16)
        grads[1, :, columns] = (nn(probs[...], mb[:, columns]) * factor).astype(jnp.bfloat16)
        for copy in grad_copies(1, head):
            copy.start()
        small_factor = factor * HEAD_SIZE ** (-0.5)
        grads[0, :, columns] = (nn(dscores[...], qb[:, columns]) * small_factor).astype(jnp.bfloat16)
        for copy in grad_copies(0, head):
            copy.start()

    def part_for(way, slot, columns):
        side = slot * LANES + (0 if way and slot else block)
        return dq_part[side : side + block, columns]

    def chunk_columns(chunk):
        return slice(chunk * wide, (chunk + 1) * wide)

    def scatter_step(hop):
        slot = slots - 1 - hop
        here = tile_out[slot]
        if hop == leap:
            after = here
        else:
            for way in range(2):
                ell_copy(way, hop).wait_recv()
            before = jnp.where(lane < block, ell_in[1, hop], ell_in[0, hop])
            top = jnp.maximum(before, here)
            after = top + jnp.log(jnp.exp(before - top) + jnp.exp(here - top))
            weights[...] = jnp.concatenate([jnp.exp(before - after), jnp.exp(here - after)], axis=0).T
        for way in range(2):
            ell_out[way, hop + 1] = after
            ell_copy(way, hop + 1).start()
        for chunk in range(CHUNKS):
            for way in range(2):
                arrives = hop != leap and chunk in chunks_of_hop(way, hop, 0)
                if arrives:
                    scattered(way, hop, chunk).wait_recv()
                side = slice(0, block) if way else slice(block, 2 * block)
                for head in range(chunk * wide // HEAD_SIZE, (chunk + 1) * wide // HEAD_SIZE):
                    columns = slice(head * HEAD_SIZE, (head + 1) * HEAD_SIZE)
                    part = part_for(way, slot, columns)
                    if hop != leap:
                        part *= weights[side, HALF_HEADS + head : HALF_HEADS + head + 1]
                    if arrives:
                        part += rs_in[way, hop, :, columns].astype(jnp.float32) * weights[side, head : head + 1]
                    rs_out[way, hop + 1, :, columns] = part.astype(jnp.bfloat16)
                scattered(way, hop + 1, chunk).start()

    for hop in range(slots):
        slot = (hop + 1) % slots
        forward(0, hop)
        if hop == 0:
            kv_own[0].wait()
            kv_sent[0].wait_recv()
        score_slot(slot)
        forward(1, hop)
        if hop == 0:
            kv_own[1].wait()
            kv_sent[1].wait_recv()
        grad_slot(slot)
        if hop == slots - 2:
            scatter_step(leap)
    ell_out[0, 0] = jnp.where(opening, tile_out[0], NEVER)
    ell_out[1, 0] = jnp.where(opening, NEVER, pltpu.roll(tile_out[0], LANES - block, 1))
    for way in range(2):
        ell_copy(way, 0).start()

    for way in range(2):
        for chunk in chunks_of_hop(way, 0, 0):
            columns = chunk_columns(chunk)
            rs_out[way, 0, :, columns] = part_for(way, 0, columns).astype(jnp.bfloat16)
            scattered(way, 0, chunk).start()

    for step in range(leap):
        scatter_step(step)
        if step == min(1, leap - 1):
            combine_logs()
        if leap + 1 + step < slots - 1:
            scatter_step(leap + 1 + step)
        if step == min(2, leap - 1):
            pass_count()
    gather_logs()
    factor = finish_count()
    for head in range(HALF_HEADS):
        grad_head(head, factor)

    for way in range(2):
        for hop in (leap, slots - 1):
            ell_copy(way, hop).wait_recv()
    sums = [(way, hop) for hop in (slots - 1, leap) for way in range(2)]
    tiles = [ell_in[way, hop] if way else pltpu.roll(ell_in[way, hop], LANES - block, 1) for way, hop in sums]
    scales = [jnp.exp(jnp.minimum(tile - log_out[...], 0.0)) for tile in (*tiles, tile_out[0], tile_out[0])]
    columns_of = [jnp.concatenate(scales[i : i + 2], axis=0).T for i in range(0, 6, 2)]
    small_factor = factor * HEAD_SIZE ** (-0.5)
    for chunk in range(CHUNKS):
        for way, hop in sums:
            scattered(way, hop, chunk).wait_recv()
        for head in range(chunk * wide // HEAD_SIZE, (chunk + 1) * wide // HEAD_SIZE):
            columns = slice(head * HEAD_SIZE, (head + 1) * HEAD_SIZE)
            total = dq_part[0:block, columns] * columns_of[2][:block, head : head + 1]
            for i, (way, hop) in enumerate(sums):
                part = rs_in[way, hop, :, columns].astype(jnp.float32)
                at = i % 2 * HALF_HEADS + head
                total += part * columns_of[i // 2][:block, at : at + 1]
            fin[:, columns] = total * small_factor
    my_rows = pl.ds(pl.multiple_of(core * rows, 8), rows)
    their_rows = pl.ds(pl.multiple_of((1 - core) * rows, 8), rows)
    last = remote(fin.at[their_rows], fin_in, fin_send, fin_recv, sibling)
    last.start()
    dq_ref[:, mine] = fin[my_rows, :]

    for copy in (*staged, count_swap, *kv_sent):
        copy.wait_send()
    for which in range(2):
        for hop in range(slots):
            for way in range(2):
                for chunk in chunks_of_hop(way, hop, slots - 1):
                    gathered(which, way, hop, chunk).wait_send()
    for hop in range(slots):
        for way in range(2):
            for chunk in chunks_of_hop(way, hop, 0):
                scattered(way, hop, chunk).wait_send()
    for hop in range(slots):
        for way in range(2):
            ell_copy(way, hop).wait_send()
        for way in delta_ways(hop):
            delta_copy(way, hop).wait_send()
    for slot in range(slots):
        for copy in tile_copies(slot):
            copy.wait_send()
    for offset in range(1, chips):
        log_copy(offset).wait_send()
    for phase, peers in enumerate((peers_x, peers_y)):
        for k, device in enumerate(peers):
            count_copy(phase, k, device).wait_send()
    for which in range(2):
        for head in range(HALF_HEADS):
            near, far = grad_copies(which, head)
            near.wait()
            far.wait()
    last.wait()
    dq_ref[:, theirs] = fin_in[...]


def hand_over(*refs):
    sources, targets, held = refs[:2], refs[3:5], refs[6:8]
    dq_in, dq_out, dq_held = refs[2], refs[5], refs[8]
    in_sems, out_sems, dq_sem = refs[9:]
    pieces = []
    for source, target, buf in zip(sources, targets, held):
        parts = 4 if source.shape[0] % 64 == 0 else 1
        size = source.shape[0] // parts
        for part in range(parts):
            rows = pl.ds(part * size, size)
            i = len(pieces)
            pieces.append(
                (
                    pltpu.make_async_copy(source.at[rows], buf.at[rows], in_sems.at[i]),
                    pltpu.make_async_copy(buf.at[rows], target.at[rows], out_sems.at[i]),
                )
            )
    dq_fetch = pltpu.make_async_copy(dq_in, dq_held, dq_sem)
    for fetch, _ in pieces:
        fetch.start()
    dq_fetch.start()
    for fetch, store in pieces:
        fetch.wait()
        store.start()
    dq_fetch.wait()
    dq_out[...] = dq_held[...].astype(dq_out.dtype)
    for _, store in pieces:
        store.wait()


def local(dp_count, queries, keys, values, attn_out, out_grad, loss_mask, input_lengths, target_lengths):
    rows, features = queries.shape[1:]
    keys_dev = keys.shape[1]
    chips = lax.axis_size("seq") // 2
    slots = chips // 2
    block = 2 * rows
    dp_x, dp_y = (4, 4) if dp_count == 16 else (1, dp_count)
    bf16, f32 = jnp.bfloat16, jnp.float32
    vmem = pl.BlockSpec(memory_space=pltpu.VMEM)
    smem = pl.BlockSpec(memory_space=pltpu.SMEM)
    anywhere = pl.BlockSpec(memory_space=pl.ANY)
    dma = pltpu.SemaphoreType.DMA
    total = chips * block * chips * 2 * keys_dev // chips * HALF
    dq, dk, dv = pl.pallas_call(
        functools.partial(kernel, dp_x, dp_y, chips),
        out_shape=(
            jax.ShapeDtypeStruct((rows, features), f32),
            jax.ShapeDtypeStruct((keys_dev, features), bf16),
            jax.ShapeDtypeStruct((keys_dev, features), bf16),
        ),
        in_specs=[smem, smem, vmem, vmem, vmem, vmem, anywhere, anywhere],
        out_specs=(vmem, anywhere, anywhere),
        scratch_shapes=[
            pltpu.VMEM((3, rows, HALF), f32),
            pltpu.VMEM((3, rows, HALF), f32),
            pltpu.VMEM((2 * keys_dev, HALF), bf16),
            pltpu.VMEM((2 * keys_dev, HALF), bf16),
            pltpu.VMEM((slots * LANES, HALF), bf16),
            pltpu.VMEM((slots * LANES, HALF), bf16),
            pltpu.VMEM((2 * keys_dev, LANES), jnp.int32),
            pltpu.VMEM((slots, HALF_HEADS, 2 * keys_dev, LANES), f32),
            pltpu.VMEM((slots, HALF_HEADS, 2 * keys_dev, LANES), f32),
            pltpu.VMEM((2 * keys_dev, slots * LANES), bf16),
            pltpu.VMEM((2 * keys_dev, slots * LANES), bf16),
            pltpu.VMEM((slots * LANES, HALF), f32),
            pltpu.VMEM((2, slots, block, HALF), bf16),
            pltpu.VMEM((2, slots, block, HALF), bf16),
            pltpu.VMEM((2, 2 * keys_dev, HALF), bf16),
            pltpu.VMEM((block, HALF), f32),
            pltpu.VMEM((rows, HALF), f32),
            pltpu.VMEM((slots, HALF_HEADS, LANES), f32),
            pltpu.VMEM((chips, HALF_HEADS, LANES), f32),
            pltpu.VMEM((HALF_HEADS, LANES), f32),
            pltpu.VMEM((chips, HALF_HEADS, LANES), f32),
            pltpu.VMEM((2, slots + 1, HALF_HEADS, LANES), f32),
            pltpu.VMEM((2, slots, HALF_HEADS, LANES), f32),
            pltpu.VMEM((2, slots, HALF_HEADS, LANES), f32),
            pltpu.VMEM((LANES, 2 * HALF_HEADS), f32),
            pltpu.VMEM((3, 8, LANES), f32),
            pltpu.VMEM((3, 3, 8, LANES), f32),
            dma((2,)),
            dma((2,)),
            dma((2,)),
            dma((4,)),
            dma((4,)),
            dma((2, 2, slots, CHUNKS)),
            dma((2, 2, slots, CHUNKS)),
            dma((2, slots, CHUNKS)),
            dma((2, slots, CHUNKS)),
            dma((chips,)),
            dma((chips,)),
            dma((chips,)),
            dma((chips,)),
            dma((2, slots)),
            dma((2, slots)),
            dma((2, slots)),
            dma((2, slots)),
            dma((2, 3)),
            dma((2, 3)),
            dma((2, HALF_HEADS)),
            dma((2, HALF_HEADS)),
            dma((2, HALF_HEADS)),
            dma,
            dma,
        ],
        compiler_params=pltpu.CompilerParams(
            collective_id=0, has_side_effects=True, vmem_limit_bytes=56 * 1024 * 1024
        ),
        cost_estimate=pl.CostEstimate(flops=10 * total, bytes_accessed=6 * 1024 * 1024, transcendentals=0),
    )(
        input_lengths[0, 0],
        target_lengths[0, 0],
        queries[0],
        out_grad[0],
        attn_out[0],
        loss_mask,
        keys[0],
        values[0],
    )
    results = (dk, dv, dq)
    dk, dv, dq = pl.pallas_call(
        hand_over,
        out_shape=tuple(jax.ShapeDtypeStruct(array.shape, bf16) for array in results),
        in_specs=[anywhere] * 3,
        out_specs=(anywhere, anywhere, vmem),
        scratch_shapes=[*(pltpu.VMEM(array.shape, array.dtype) for array in results), dma((8,)), dma((8,)), dma],
        compiler_params=pltpu.CompilerParams(vmem_limit_bytes=56 * 1024 * 1024),
        cost_estimate=pl.CostEstimate(flops=0, bytes_accessed=5 * 1024 * 1024, transcendentals=0),
    )(*results)
    return dq[None], dk[None], dv[None]


def solution(mesh):
    return jax.shard_map(
        functools.partial(local, mesh.shape["dp"]),
        mesh=mesh,
        in_specs=(
            P("dp", "seq", None),
            P("dp", "seq", None),
            P("dp", "seq", None),
            P("dp", "seq", None),
            P("dp", "seq", None),
            P("dp", "seq"),
            P("dp", None, None),
            P("dp", None, None),
        ),
        out_specs=(P("dp", "seq", None), P("dp", "seq", None), P("dp", "seq", None)),
        check_vma=False,
    )
```
